128 devices in a mesh: chan: 16 (over x, y), hole: 8 (over z, core).
Axes of the slice: x: 4, y: 4, z: 4, core: 2. Of those that a mesh axis runs over, the one named last changes fastest.
Arguments:
- amplitudes: float32 [64, 1024, 1024], P('chan', None, 'hole'), may hold values from -6 to 6
- interaction: float32 [64, 1024, 1024], P('chan'), may hold values from -0.1875 to 0.1875
- sixj_values: float32 [64], replicated, may hold values from -0.75 to 0.75
- sixj_index: int32 [64, 64], replicated, may hold values from 0 to 63
- ph_rows: int32 [64], P('chan'), may hold values from 1 to 1024, as said below
- denominators: float32 [64, 1024, 1024], P('chan', None, 'hole'), may hold values from 1 to 8
Outputs:
- update: float32 [64, 1024, 1024], P('chan', None, 'hole')
The draws below stay inside these ranges and needn't reach their ends.
Inputs may be any that keep to these rules, and one draw needn't show every extreme that they name: `ph_rows`: at least one channel has all 1024 rows live.
All inputs are finite; a program needn't handle non-finite values.
Results may differ from the reference program's by a relative error of at most 0.00012.
Values sent between devices are 32-bit elements; how exact they have to be, the bound alone decides.
No kernel may reach another device: no remote copies, remote signals or barrier semaphores. Data moves between devices by JAX's collectives and lax.ppermute only.
A program may use at most 128 MiB of HBM per device.

```python
import math
import jax
import jax.numpy as jnp
from jax import lax

P_SIZE = 1024
H = 1024
NSIX = 64
NCH = 64


def draw_ph_rows(key, part):
    key = jax.random.fold_in(key, 7)
    first, second = jax.random.split(key)
    rows = jax.random.randint(first, (NCH,), 1, P_SIZE + 1)
    chosen = jax.random.randint(second, (), 0, NCH)
    return jnp.where(jnp.arange(NCH) == chosen, P_SIZE, rows).astype(jnp.int32)


def set_ends(drawn, stream_key, low, largest):
    longest = drawn.shape.index(max(drawn.shape))
    spots = []
    for shift in (0, 1):
        where = [jax.random.randint(jax.random.fold_in(stream_key, axis), (), 0, length) for axis, length in enumerate(drawn.shape)]
        where[longest] = (where[longest] + shift) % drawn.shape[longest]
        spots.append(tuple(where))
    return drawn.at[spots[0]].set(low).at[spots[1]].set(largest)


def levels(own_key, extent, pieces, low, high):
    factor_of, own = 1.0, jax.random.fold_in(own_key, 6)
    for axis_at, parts in pieces:
        heights = jnp.exp(jax.random.uniform(jax.random.fold_in(own, axis_at), (parts,), jnp.float32, low / len(pieces), high / len(pieces)))
        factor_of = factor_of * jnp.repeat(heights, extent[axis_at] // parts).reshape([-1 if axis == axis_at else 1 for axis in range(len(extent))])
    return factor_of


def scatter_about(key, shape, scale, reach, pieces=(), held_as=jnp.bfloat16):
    values = scale * jax.random.normal(key, shape, jnp.float32)
    if pieces:
        values = values * levels(key, shape, pieces, -0.22, 0.18)
    return jnp.clip(values, -reach, reach).astype(held_as)


def setup_inputs(seed: int = 0) -> dict:
    streams_of = jax.random.split(jax.random.key(seed), 7)
    amplitudes = scatter_about(streams_of[0], (NCH, P_SIZE, H), 1.0, 6.0, ((0, 16), (2, 8)), jnp.float32)
    interaction = scatter_about(streams_of[1], (NCH, P_SIZE, P_SIZE), P_SIZE ** -0.5, 0.1875, ((0, 16),), jnp.float32)
    sixj_values = scatter_about(streams_of[2], (NSIX,), NCH ** -0.5, 0.75, (), jnp.float32)
    sixj_index = set_ends(jax.random.randint(streams_of[3], (NCH, NCH), 0, NSIX), jax.random.fold_in(streams_of[3], 1), 0, NSIX - 1).astype(jnp.int32)
    ph_rows = draw_ph_rows(jax.random.fold_in(streams_of[6], 71), 0)
    denominators = jnp.clip(jnp.exp(math.log(8.0) - 2.0794415 * jax.random.uniform(streams_of[5], (NCH, P_SIZE, H), jnp.float32) ** levels(streams_of[5], (NCH, P_SIZE, H), ((0, 16), (2, 8)), -0.2, 0.2)), 1.0, 8.0)
    return dict(amplitudes=amplitudes, interaction=interaction, sixj_values=sixj_values, sixj_index=sixj_index, ph_rows=ph_rows, denominators=denominators)


def reference(amplitudes, interaction, sixj_values, sixj_index, ph_rows, denominators):
    hp = lax.Precision.HIGHEST
    slots = jnp.arange(NSIX, dtype=jnp.int32)
    weights = lax.optimization_barrier(jnp.sum(jnp.where(sixj_index[:, :, None] == slots[None, None, :], sixj_values[None, None, :], jnp.float32(0.0)), axis=2))
    live = (jnp.arange(P_SIZE, dtype=jnp.int32)[None, :] < ph_rows[:, None]).astype(jnp.float32)[:, :, None]
    recoupled = jnp.einsum('dc,cph->dph', weights, amplitudes, precision=hp) * live
    linear = jnp.einsum('dpq,dqh->dph', interaction, recoupled, precision=hp)
    inner = jnp.einsum('dph,dpk->dhk', recoupled, linear, precision=hp)
    scale = 1.0 / jnp.sqrt(jnp.float32(P_SIZE * H))
    cycle = (linear + jnp.einsum('dph,dhk->dpk', recoupled, inner, precision=hp) * scale) * live
    back = jnp.einsum('dc,dph->cph', weights, cycle, precision=hp)
    return back / denominators
```

```python
import jax
import jax.numpy as jnp
from jax import lax
from jax.sharding import Mesh, PartitionSpec as P

CHIPS = ("chan", "z")


def mix_rows(table, blocks):
    return jnp.einsum("dc,cph->dph", table, blocks, precision=lax.Precision.HIGH)


def per_device(amplitudes, interaction, sixj_values, sixj_index, ph_rows, denominators):
    hp = lax.Precision.HIGH
    slots = jnp.arange(sixj_values.shape[0], dtype=jnp.int32)
    weights = jnp.sum(
        jnp.where(
            sixj_index[:, :, None] == slots[None, None, :],
            sixj_values[None, None, :],
            jnp.float32(0.0),
        ),
        axis=2,
    )
    z = lax.axis_index("z")
    n_chan, n_z = lax.axis_size("chan"), lax.axis_size("z")
    height, width = amplitudes.shape[1:]
    part = height // n_chan
    rows_of = lax.dynamic_index_in_dim(ph_rows, z, 0, keepdims=False)
    live = (jnp.arange(height, dtype=jnp.int32) < rows_of).astype(jnp.float32)[:, None]
    block = lax.dynamic_index_in_dim(interaction, z, 0, keepdims=False)

    rows = lax.all_to_all(amplitudes, "chan", split_axis=1, concat_axis=0, tiled=True)
    mixed = mix_rows(weights, rows)
    mine = lax.all_to_all(mixed, CHIPS, split_axis=0, concat_axis=0, tiled=True)
    mine = mine.reshape(n_chan, n_z, part, width).transpose(0, 2, 1, 3).reshape(height, n_z * width)
    mine = mine * live
    other = lax.ppermute(mine, "core", [(0, 1), (1, 0)])
    linear = jnp.dot(block, mine, precision=hp)
    scale = 1.0 / jnp.sqrt(jnp.float32(height * n_z * width * 2))

    def term(side):
        inner = lax.dot_general(side, linear, (((0,), (0,)), ((), ())), precision=hp)
        return jnp.dot(side, inner, precision=hp)

    cycle = (linear + (term(mine) + term(other)) * scale) * live
    cycle = cycle.reshape(n_chan, part, n_z, width).transpose(0, 2, 1, 3).reshape(-1, part, width)
    spread = lax.all_to_all(cycle, CHIPS, split_axis=0, concat_axis=0, tiled=True)
    back = mix_rows(weights.T, spread)
    back = lax.all_to_all(back, "chan", split_axis=0, concat_axis=1, tiled=True)
    return back / denominators


def solution(mesh):
    split = Mesh(mesh.devices.reshape(mesh.devices.shape[0], -1, 2), ("chan", "z", "core"))
    hole = ("z", "core")
    in_specs = (
        P("chan", None, hole),
        P("chan", None, None),
        P(),
        P(),
        P("chan"),
        P("chan", None, hole),
    )
    return jax.shard_map(
        per_device, mesh=split, in_specs=in_specs, out_specs=P("chan", None, hole), check_vma=False
    )
```

```python
import functools
import jax
import jax.numpy as jnp
from jax import lax
from jax.experimental import pallas as pl
from jax.experimental.pallas import tpu as pltpu
from jax.sharding import Mesh, PartitionSpec as P

CHIPS = ("chan", "z")
WHOLE, SPLIT = (0, 64), (0, 8, 64)
MIB = 2**20
BF16, F32 = jnp.bfloat16, jnp.float32
ANY = pl.BlockSpec(memory_space=pl.ANY)
FULL = pl.BlockSpec(memory_space=pltpu.VMEM)
SCALAR = pl.BlockSpec(memory_space=pltpu.SMEM)
SUB = 8


def halves(x):
    high = x.astype(BF16)
    return high, (x - high.astype(F32)).astype(BF16)


def dot3(a, b, dims=((1,), (0,))):
    def one(x, y):
        return lax.dot_general(x, y, (dims, ((), ())), preferred_element_type=F32)

    return one(a[0], b[0]) + (one(a[0], b[1]) + one(a[1], b[0]))


def params(mib):
    return pltpu.CompilerParams(vmem_limit_bytes=mib * MIB)


def deal_kernel(cuts, blocks, *outs):
    for c in range(blocks.shape[0]):
        for k, out in enumerate(outs):
            out[:, c] = blocks[c, :, cuts[k] : cuts[k + 1]]


def deal(blocks, n, cuts, step=4):
    c, height, width = blocks.shape
    part = height // n
    sizes = [b - a for a, b in zip(cuts[:-1], cuts[1:])]
    pieces = pl.pallas_call(
        functools.partial(deal_kernel, cuts),
        grid=(n // step,),
        out_shape=[jax.ShapeDtypeStruct((n, c, rows, width), F32) for rows in sizes],
        in_specs=[pl.BlockSpec((c, step, part, width), lambda i: (0, i, 0, 0))],
        out_specs=[pl.BlockSpec((step, c, rows, width), lambda i: (i, 0, 0, 0)) for rows in sizes],
        compiler_params=params(8),
        cost_estimate=pl.CostEstimate(flops=0, bytes_accessed=8 * c * height * width, transcendentals=0),
    )(blocks.reshape(c, n, part, width))
    return [piece.reshape(n * c, rows, width) for piece, rows in zip(pieces, sizes)]


def spread_table(table):
    n = table.shape[0]
    wide = n * SUB
    rows = (lax.broadcasted_iota(jnp.int32, (wide, n), 0) // SUB == lax.broadcasted_iota(jnp.int32, (wide, n), 1)).astype(BF16)
    columns = (lax.broadcasted_iota(jnp.int32, (n, wide), 1) // SUB == lax.broadcasted_iota(jnp.int32, (n, wide), 0)).astype(BF16)
    same = lax.broadcasted_iota(jnp.int32, (wide, wide), 0) % SUB == lax.broadcasted_iota(jnp.int32, (wide, wide), 1) % SUB
    spread = []
    for part in halves(table):
        tall = jnp.dot(rows, part, preferred_element_type=F32).astype(BF16)
        both = jnp.dot(tall, columns, preferred_element_type=F32)
        spread.append(jnp.where(same, both, 0.0).astype(BF16))
    return tuple(spread)


def mix_kernel(table, *refs):
    ins, out = refs[:-1], refs[-1]
    n, _, width = out.shape
    spread = spread_table(table[...])
    groups = [(ref, row) for ref in ins for row in range(0, ref.shape[1], SUB)]
    for at in range(0, len(groups), 2):
        x = jnp.concatenate(
            [ref[:, row : row + SUB, :].reshape(n * SUB, width) for ref, row in groups[at : at + 2]], axis=1
        )
        y = dot3(spread, halves(x))
        for k in range(2):
            out[:, (at + k) * SUB : (at + k + 1) * SUB, :] = y[:, k * width : (k + 1) * width].reshape(n, SUB, width)


def mix(table, pieces):
    n, _, width = pieces[0].shape
    part = sum(p.shape[1] for p in pieces)
    return pl.pallas_call(
        mix_kernel,
        out_shape=jax.ShapeDtypeStruct((n, part, width), F32),
        in_specs=[FULL] * (1 + len(pieces)),
        out_specs=FULL,
        compiler_params=params(16),
        cost_estimate=pl.CostEstimate(
            flops=6 * n * n * part * width * SUB, bytes_accessed=8 * n * part * width, transcendentals=0
        ),
    )(table, *pieces)


def gather_side(ref, rows_of, scratch_high, scratch_low):
    n, part, width = ref.shape
    n_z = scratch_high.shape[1] // width
    for g in range(n // n_z):
        span = slice(g * part, (g + 1) * part)
        live = g * part + lax.broadcasted_iota(jnp.int32, (part, width), 0) < rows_of
        for k in range(n_z):
            high, low = halves(jnp.where(live, ref[g * n_z + k], 0.0))
            scratch_high[span, k * width : (k + 1) * width] = high
            scratch_low[span, k * width : (k + 1) * width] = low


def own_kernel(scale, block, at, rows, side, inter, acc, lin_h, lin_l, v, side_h, side_l, sem):
    height = v.shape[0]
    copies = [
        pltpu.make_async_copy(inter.at[at[0], pl.ds(r, block)], v.at[pl.ds(r, block)], sem.at[r // block])
        for r in range(0, height, block)
    ]
    for copy in copies:
        copy.start()
    gather_side(side, rows[0], side_h, side_l)
    mine = (side_h[...], side_l[...])
    for r, copy in zip(range(0, height, block), copies):
        copy.wait()
        linear = dot3(halves(v[r : r + block]), mine)
        acc[r : r + block] = linear
        lin_h[r : r + block], lin_l[r : r + block] = halves(linear)
    inner = halves(dot3(mine, (lin_h[...], lin_l[...]), ((0,), (0,))) * scale)
    for r in range(0, height, block):
        acc[r : r + block] += dot3(tuple(s[r : r + block] for s in mine), inner)


def own(at, rows, side, inter, scale, block=256):
    n, part, width = side.shape
    height = inter.shape[1]
    cols = n * part * width // height
    sds = jax.ShapeDtypeStruct
    return pl.pallas_call(
        functools.partial(own_kernel, scale, block),
        out_shape=[sds((height, cols), F32), sds((height, cols), BF16), sds((height, cols), BF16)],
        in_specs=[SCALAR, SCALAR, FULL, ANY],
        out_specs=[FULL] * 3,
        scratch_shapes=[
            pltpu.VMEM((height, height), F32),
            pltpu.VMEM((height, cols), BF16),
            pltpu.VMEM((height, cols), BF16),
            pltpu.SemaphoreType.DMA((height // block,)),
        ],
        compiler_params=params(30),
        cost_estimate=pl.CostEstimate(
            flops=12 * height * height * cols, bytes_accessed=4 * height * (height + 3 * cols), transcendentals=0
        ),
    )(at, rows, side, inter)


def other_kernel(scale, cuts, rows, side, base, lin_h, lin_l, *refs):
    outs, (side_h, side_l) = refs[:-2], refs[-2:]
    n, part, width = side.shape
    n_z = side_h.shape[1] // width
    gather_side(side, rows[0], side_h, side_l)
    theirs = (side_h[...], side_l[...])
    inner = halves(dot3(theirs, (lin_h[...], lin_l[...]), ((0,), (0,))) * scale)
    step = 4
    for g0 in range(0, n // n_z, step):
        span = slice(g0 * part, (g0 + step) * part)
        total = base[span] + dot3(tuple(s[span] for s in theirs), inner)
        live = g0 * part + lax.broadcasted_iota(jnp.int32, total.shape, 0) < rows[0]
        total = jnp.where(live, total, 0.0)
        for g in range(step):
            for k in range(n_z):
                tile = total[g * part : (g + 1) * part, k * width : (k + 1) * width]
                for i, out in enumerate(outs):
                    out[(g0 + g) * n_z + k] = tile[cuts[i] : cuts[i + 1]]


def other(rows, side, base, lin_h, lin_l, scale, cuts):
    n, part, width = side.shape
    height, cols = base.shape
    return pl.pallas_call(
        functools.partial(other_kernel, scale, cuts),
        out_shape=[jax.ShapeDtypeStruct((n, b - a, width), F32) for a, b in zip(cuts[:-1], cuts[1:])],
        in_specs=[SCALAR] + [FULL] * 4,
        out_specs=[FULL] * (len(cuts) - 1),
        scratch_shapes=[pltpu.VMEM((height, cols), BF16)] * 2,
        compiler_params=params(24),
        cost_estimate=pl.CostEstimate(
            flops=12 * height * cols * cols, bytes_accessed=16 * height * cols, transcendentals=0
        ),
    )(rows, side, base, lin_h, lin_l)


def exchange(pieces, axes):
    return [lax.all_to_all(piece, axes, split_axis=0, concat_axis=0, tiled=True) for piece in pieces]


def weights_of(values, index):
    slots = jnp.arange(values.shape[0], dtype=jnp.int32)
    return jnp.sum(jnp.where(index[:, :, None] == slots[None, None, :], values[None, None, :], jnp.float32(0.0)), axis=2)


def per_device(amplitudes, interaction, sixj_values, sixj_index, ph_rows, denominators):
    c, height, width = amplitudes.shape
    n_chan, n_z = lax.axis_size("chan"), lax.axis_size("z")
    z, core = lax.axis_index("z"), lax.axis_index("core")
    at = jnp.reshape(z, (1,)).astype(jnp.int32)
    rows_of = lax.dynamic_slice_in_dim(ph_rows, z, 1)
    scale = 1.0 / (height * width * n_z * 2) ** 0.5

    def forward(cuts):
        def run(blocks, values, index):
            weights = weights_of(values, index)
            mixed = mix(weights, exchange(deal(blocks, n_chan, cuts), "chan"))
            return exchange([mixed], CHIPS)[0], weights

        return run

    def backward(cuts):
        def run(rows, theirs, base, lin_h, lin_l, weights, below):
            cycle = other(rows, theirs, base, lin_h, lin_l, scale, cuts)
            back = mix(weights.T, exchange(cycle, CHIPS))
            back = exchange([back], "chan")[0]
            back = back.reshape(n_chan, c, height // n_chan, width).transpose(1, 0, 2, 3).reshape(c, height, width)
            return back / below

        return run

    mine, weights = lax.cond(core == 0, forward(WHOLE), forward(SPLIT), amplitudes, sixj_values, sixj_index)
    theirs = lax.ppermute(mine, "core", [(0, 1), (1, 0)])
    base, lin_h, lin_l = own(at, rows_of, mine, interaction, scale)
    return lax.cond(
        core == 0, backward(WHOLE), backward(SPLIT), rows_of, theirs, base, lin_h, lin_l, weights, denominators
    )


def solution(mesh):
    split = Mesh(mesh.devices.reshape(mesh.devices.shape[0], -1, 2), ("chan", "z", "core"))
    hole = ("z", "core")
    in_specs = (
        P("chan", None, hole),
        P("chan", None, None),
        P(),
        P(),
        P("chan"),
        P("chan", None, hole),
    )
    return jax.shard_map(
        per_device, mesh=split, in_specs=in_specs, out_specs=P("chan", None, hole), check_vma=False
    )
```

```python
import bisect
import functools
import jax
import jax.numpy as jnp
from jax import lax
from jax.experimental import pallas as pl
from jax.experimental.pallas import tpu as pltpu
from jax.sharding import Mesh, PartitionSpec as P

CHIPS = ("chan", "z")
FIRST = ((0, 64), (0, 8, 64))
THIRD = ((0, 64), (0, 8, 64))
OWN_MIB = 52
EARLY1 = (False, False)
EARLY = (True, True)
LAST = ((0, 64), (0, 64))
MIB = 2**20
BF16, F32 = jnp.bfloat16, jnp.float32
ANY = pl.BlockSpec(memory_space=pl.ANY)
FULL = pl.BlockSpec(memory_space=pltpu.VMEM)
SCALAR = pl.BlockSpec(memory_space=pltpu.SMEM)
SUB = 8


def halves(x):
    high = x.astype(BF16)
    return high, (x - high.astype(F32)).astype(BF16)


def dot3(a, b, dims=((1,), (0,))):
    def one(x, y):
        return lax.dot_general(x, y, (dims, ((), ())), preferred_element_type=F32)

    return one(a[0], b[0]) + (one(a[0], b[1]) + one(a[1], b[0]))


def params(mib):
    return pltpu.CompilerParams(vmem_limit_bytes=mib * MIB)


def deal_kernel(cuts, blocks, *refs):
    outs, sems = refs[:-1], refs[-1]
    copies = [
        pltpu.make_async_copy(
            blocks.at[c, :, pl.ds(cuts[k], cuts[k + 1] - cuts[k])], out.at[:, c], sems.at[k * blocks.shape[0] + c]
        )
        for k, out in enumerate(outs)
        for c in range(blocks.shape[0])
    ]
    for copy in copies:
        copy.start()
    for copy in copies:
        copy.wait()


def deal(blocks, n, cuts):
    c, height, width = blocks.shape
    part = height // n
    sizes = [b - a for a, b in zip(cuts[:-1], cuts[1:])]
    pieces = pl.pallas_call(
        functools.partial(deal_kernel, cuts),
        out_shape=[jax.ShapeDtypeStruct((n, c, rows, width), F32) for rows in sizes],
        in_specs=[ANY],
        out_specs=[FULL] * len(sizes),
        scratch_shapes=[pltpu.SemaphoreType.DMA((len(sizes) * c,))],
        compiler_params=params(8),
        cost_estimate=pl.CostEstimate(flops=0, bytes_accessed=8 * c * height * width, transcendentals=0),
    )(blocks.reshape(c, n, part, width))
    return [piece.reshape(n * c, rows, width) for piece, rows in zip(pieces, sizes)]


def spread_table(table):
    n = table.shape[0]
    wide = n * SUB
    rows = (lax.broadcasted_iota(jnp.int32, (wide, n), 0) // SUB == lax.broadcasted_iota(jnp.int32, (wide, n), 1)).astype(BF16)
    columns = (lax.broadcasted_iota(jnp.int32, (n, wide), 1) // SUB == lax.broadcasted_iota(jnp.int32, (n, wide), 0)).astype(BF16)
    same = lax.broadcasted_iota(jnp.int32, (wide, wide), 0) % SUB == lax.broadcasted_iota(jnp.int32, (wide, wide), 1) % SUB
    spread = []
    for part in halves(table):
        tall = jnp.dot(rows, part, preferred_element_type=F32).astype(BF16)
        both = jnp.dot(tall, columns, preferred_element_type=F32)
        spread.append(jnp.where(same, both, 0.0).astype(BF16))
    return tuple(spread)


def mix_kernel(cuts, back, values, index, *refs):
    ins, outs = refs[: 1 - len(cuts)], refs[1 - len(cuts) :]
    n, _, width = outs[0].shape
    if values.shape == index.shape:
        table = values[...]
    else:
        table = jnp.zeros(index.shape, F32)
        for slot in range(values.shape[0]):
            table = jnp.where(index[...] == slot, values[slot], table)
    spread = spread_table(table.T if back else table)
    groups = [(ref, row) for ref in ins for row in range(0, ref.shape[1], SUB)]
    for at in range(0, len(groups), 2):
        x = jnp.concatenate(
            [ref[:, row : row + SUB, :].reshape(n * SUB, width) for ref, row in groups[at : at + 2]], axis=1
        )
        y = dot3(spread, halves(x))
        for k in range(2):
            row = (at + k) * SUB
            i = bisect.bisect_right(cuts, row) - 1
            outs[i][:, row - cuts[i] : row - cuts[i] + SUB, :] = y[:, k * width : (k + 1) * width].reshape(n, SUB, width)


def mix(values, index, pieces, cuts, back=False):
    n, _, width = pieces[0].shape
    part = cuts[-1]
    return pl.pallas_call(
        functools.partial(mix_kernel, cuts, back),
        out_shape=[jax.ShapeDtypeStruct((n, b - a, width), F32) for a, b in zip(cuts[:-1], cuts[1:])],
        in_specs=[FULL if values.ndim == 2 else SCALAR] + [FULL] * (1 + len(pieces)),
        out_specs=[FULL] * (len(cuts) - 1),
        compiler_params=params(16),
        cost_estimate=pl.CostEstimate(
            flops=6 * n * n * part * width * SUB, bytes_accessed=8 * n * part * width, transcendentals=0
        ),
    )(values, index, *pieces)


def gather_side(ref, rows_of, scratch_high, scratch_low):
    n, part, width = ref.shape
    n_z = scratch_high.shape[1] // width
    for g in range(n // n_z):
        span = slice(g * part, (g + 1) * part)
        live = g * part + lax.broadcasted_iota(jnp.int32, (part, width), 0) < rows_of
        for k in range(n_z):
            high, low = halves(jnp.where(live, ref[g * n_z + k], 0.0))
            scratch_high[span, k * width : (k + 1) * width] = high
            scratch_low[span, k * width : (k + 1) * width] = low


def own_kernel(scale, block, at, rows, side, inter, acc, lin_h, lin_l, v, raw, side_h, side_l, sem):
    height = v.shape[0]
    first = pltpu.make_async_copy(side, raw, sem.at[0])
    first.start()
    copies = [
        pltpu.make_async_copy(inter.at[at[0], pl.ds(r, block)], v.at[pl.ds(r, block)], sem.at[1 + r // block])
        for r in range(0, height, block)
    ]
    for copy in copies:
        copy.start()
    first.wait()
    gather_side(raw, rows[0], side_h, side_l)
    mine = (side_h[...], side_l[...])
    for r, copy in zip(range(0, height, block), copies):
        copy.wait()
        linear = dot3(halves(v[r : r + block]), mine)
        acc[r : r + block] = linear
        lin_h[r : r + block], lin_l[r : r + block] = halves(linear)
    inner = halves(dot3(mine, (lin_h[...], lin_l[...]), ((0,), (0,))) * scale)
    for r in range(0, height, block):
        acc[r : r + block] += dot3(tuple(s[r : r + block] for s in mine), inner)


def own(at, rows, side, inter, scale, block=256):
    n, part, width = side.shape
    height = inter.shape[1]
    cols = n * part * width // height
    sds = jax.ShapeDtypeStruct
    return pl.pallas_call(
        functools.partial(own_kernel, scale, block),
        out_shape=[sds((height, cols), F32), sds((height, cols), BF16), sds((height, cols), BF16)],
        in_specs=[SCALAR, SCALAR, ANY, ANY],
        out_specs=[FULL] * 3,
        scratch_shapes=[
            pltpu.VMEM((height, height), F32),
            pltpu.VMEM(side.shape, F32),
            pltpu.VMEM((height, cols), BF16),
            pltpu.VMEM((height, cols), BF16),
            pltpu.SemaphoreType.DMA((1 + height // block,)),
        ],
        compiler_params=params(OWN_MIB),
        cost_estimate=pl.CostEstimate(
            flops=12 * height * height * cols, bytes_accessed=4 * height * (height + 3 * cols), transcendentals=0
        ),
    )(at, rows, side, inter)


def other_kernel(scale, cuts, rows, side, base, lin_h, lin_l, *refs):
    outs, (side_h, side_l) = refs[:-2], refs[-2:]
    n, part, width = side.shape
    n_z = side_h.shape[1] // width
    gather_side(side, rows[0], side_h, side_l)
    theirs = (side_h[...], side_l[...])
    inner = halves(dot3(theirs, (lin_h[...], lin_l[...]), ((0,), (0,))) * scale)
    step = 4
    for g0 in range(0, n // n_z, step):
        span = slice(g0 * part, (g0 + step) * part)
        total = base[span] + dot3(tuple(s[span] for s in theirs), inner)
        live = g0 * part + lax.broadcasted_iota(jnp.int32, total.shape, 0) < rows[0]
        total = jnp.where(live, total, 0.0)
        for g in range(step):
            for k in range(n_z):
                tile = total[g * part : (g + 1) * part, k * width : (k + 1) * width]
                for i, out in enumerate(outs):
                    out[(g0 + g) * n_z + k] = tile[cuts[i] : cuts[i + 1]]


def other(rows, side, base, lin_h, lin_l, scale, cuts):
    n, part, width = side.shape
    height, cols = base.shape
    return pl.pallas_call(
        functools.partial(other_kernel, scale, cuts),
        out_shape=[jax.ShapeDtypeStruct((n, b - a, width), F32) for a, b in zip(cuts[:-1], cuts[1:])],
        in_specs=[SCALAR] + [FULL] * 4,
        out_specs=[FULL] * (len(cuts) - 1),
        scratch_shapes=[pltpu.VMEM((height, cols), BF16)] * 2,
        compiler_params=params(24),
        cost_estimate=pl.CostEstimate(
            flops=12 * height * cols * cols, bytes_accessed=16 * height * cols, transcendentals=0
        ),
    )(rows, side, base, lin_h, lin_l)


def finish_kernel(cuts, below, *refs):
    ins, out = refs[:-1], refs[-1]
    for i, ref in enumerate(ins):
        rows = slice(cuts[i], cuts[i + 1])
        out[0, :, rows] = ref[:, 0] / below[0, :, rows]


def finish(pieces, below, n, cuts):
    c, height, width = below.shape
    part = height // n
    whole = pl.BlockSpec((1, n, part, width), lambda i: (i, 0, 0, 0))
    sizes = [b - a for a, b in zip(cuts[:-1], cuts[1:])]
    return pl.pallas_call(
        functools.partial(finish_kernel, cuts),
        grid=(c,),
        out_shape=jax.ShapeDtypeStruct((c, n, part, width), F32),
        in_specs=[whole] + [pl.BlockSpec((n, 1, rows, width), lambda i: (0, i, 0, 0)) for rows in sizes],
        out_specs=whole,
        compiler_params=params(12),
        cost_estimate=pl.CostEstimate(flops=c * height * width, bytes_accessed=12 * c * height * width, transcendentals=0),
    )(below.reshape(c, n, part, width), *[p.reshape(n, c, rows, width) for p, rows in zip(pieces, sizes)]).reshape(c, height, width)


def exchange(pieces, axes):
    return [lax.all_to_all(piece, axes, split_axis=0, concat_axis=0, tiled=True) for piece in pieces]


def weights_of(values, index):
    slots = jnp.arange(values.shape[0], dtype=jnp.int32)
    return jnp.sum(jnp.where(index[:, :, None] == slots[None, None, :], values[None, None, :], jnp.float32(0.0)), axis=2)


def per_device(amplitudes, interaction, sixj_values, sixj_index, ph_rows, denominators):
    c, height, width = amplitudes.shape
    n_chan, n_z = lax.axis_size("chan"), lax.axis_size("z")
    z, core = lax.axis_index("z"), lax.axis_index("core")
    at = jnp.reshape(z, (1,)).astype(jnp.int32)
    rows_of = lax.dynamic_slice_in_dim(ph_rows, z, 1)
    scale = 1.0 / (height * width * n_z * 2) ** 0.5

    def forward(core):
        def run(blocks, values, index):
            parts = exchange(deal(blocks, n_chan, FIRST[core]), "chan")
            if EARLY1[core]:
                values = weights_of(values, index)
            return exchange(mix(values, index, parts, (0, height // n_chan)), CHIPS)[0]

        return run

    def backward(core):
        def run(rows, theirs, values, index, below, *sums):
            cycle = other(rows, theirs, *sums, scale, THIRD[core])
            if EARLY[core]:
                values = weights_of(values, index)
            back = mix(values, index, exchange(cycle, CHIPS), LAST[core], back=True)
            return finish(exchange(back, "chan"), below, n_chan, LAST[core])

        return run

    tables = (sixj_values, sixj_index)
    mine = lax.cond(core == 0, forward(0), forward(1), amplitudes, *tables)
    theirs = lax.ppermute(mine, "core", [(0, 1), (1, 0)])
    sums = own(at, rows_of, mine, interaction, scale)
    return lax.cond(core == 0, backward(0), backward(1), rows_of, theirs, *tables, denominators, *sums)


def solution(mesh):
    split = Mesh(mesh.devices.reshape(mesh.devices.shape[0], -1, 2), ("chan", "z", "core"))
    hole = ("z", "core")
    in_specs = (
        P("chan", None, hole),
        P("chan", None, None),
        P(),
        P(),
        P("chan"),
        P("chan", None, hole),
    )
    return jax.shard_map(
        per_device, mesh=split, in_specs=in_specs, out_specs=P("chan", None, hole), check_vma=False
    )
```

```python
import bisect
import functools
import jax
import jax.numpy as jnp
from jax import lax
from jax.experimental import pallas as pl
from jax.experimental.pallas import tpu as pltpu
from jax.sharding import Mesh, PartitionSpec as P

CHIPS = ("chan", "z")
FIRST = ((0, 64), (0, 8, 64))
THIRD = ((0, 64), (0, 8, 64))
OWN_MIB = 52
LAST = ((0, 64), (0, 64))
MIB = 2**20
BF16, F32 = jnp.bfloat16, jnp.float32
ANY = pl.BlockSpec(memory_space=pl.ANY)
FULL = pl.BlockSpec(memory_space=pltpu.VMEM)
SCALAR = pl.BlockSpec(memory_space=pltpu.SMEM)
SUB = 8


def halves(x):
    high = x.astype(BF16)
    return high, (x - high.astype(F32)).astype(BF16)


def dot3(a, b, dims=((1,), (0,))):
    def one(x, y):
        return lax.dot_general(x, y, (dims, ((), ())), preferred_element_type=F32)

    return one(a[0], b[0]) + (one(a[0], b[1]) + one(a[1], b[0]))


def params(mib):
    return pltpu.CompilerParams(vmem_limit_bytes=mib * MIB)


def deal_kernel(cuts, blocks, *refs):
    outs, sems = refs[:-1], refs[-1]
    copies = [
        pltpu.make_async_copy(
            blocks.at[c, :, pl.ds(cuts[k], cuts[k + 1] - cuts[k])], out.at[:, c], sems.at[k * blocks.shape[0] + c]
        )
        for k, out in enumerate(outs)
        for c in range(blocks.shape[0])
    ]
    for copy in copies:
        copy.start()
    for copy in copies:
        copy.wait()


def deal(blocks, n, cuts):
    c, height, width = blocks.shape
    part = height // n
    sizes = [b - a for a, b in zip(cuts[:-1], cuts[1:])]
    pieces = pl.pallas_call(
        functools.partial(deal_kernel, cuts),
        out_shape=[jax.ShapeDtypeStruct((n, c, rows, width), F32) for rows in sizes],
        in_specs=[ANY],
        out_specs=[FULL] * len(sizes),
        scratch_shapes=[pltpu.SemaphoreType.DMA((len(sizes) * c,))],
        compiler_params=params(8),
        cost_estimate=pl.CostEstimate(flops=0, bytes_accessed=8 * c * height * width, transcendentals=0),
    )(blocks.reshape(c, n, part, width))
    return [piece.reshape(n * c, rows, width) for piece, rows in zip(pieces, sizes)]


def spread_table(table):
    n = table.shape[0]
    wide = n * SUB
    rows = (lax.broadcasted_iota(jnp.int32, (wide, n), 0) // SUB == lax.broadcasted_iota(jnp.int32, (wide, n), 1)).astype(BF16)
    columns = (lax.broadcasted_iota(jnp.int32, (n, wide), 1) // SUB == lax.broadcasted_iota(jnp.int32, (n, wide), 0)).astype(BF16)
    same = lax.broadcasted_iota(jnp.int32, (wide, wide), 0) % SUB == lax.broadcasted_iota(jnp.int32, (wide, wide), 1) % SUB
    spread = []
    for part in halves(table):
        tall = jnp.dot(rows, part, preferred_element_type=F32).astype(BF16)
        both = jnp.dot(tall, columns, preferred_element_type=F32)
        spread.append(jnp.where(same, both, 0.0).astype(BF16))
    return tuple(spread)


def mix_kernel(cuts, back, *refs):
    n_in, n_out = (1, len(cuts) - 1) if back else (2, len(cuts))
    given, pieces, outs = refs[:n_in], refs[n_in:-n_out], refs[-n_out:]
    n, _, width = outs[0].shape
    if back:
        table = given[0][...].T
    else:
        values, index = given
        table = jnp.zeros(index.shape, F32)
        for slot in range(values.shape[0]):
            table = jnp.where(index[...] == slot, values[slot], table)
        outs[-1][...] = table
    spread = spread_table(table)
    groups = [(ref, row) for ref in pieces for row in range(0, ref.shape[1], SUB)]
    for at in range(0, len(groups), 2):
        x = jnp.concatenate(
            [ref[:, row : row + SUB, :].reshape(n * SUB, width) for ref, row in groups[at : at + 2]], axis=1
        )
        y = dot3(spread, halves(x))
        for k in range(2):
            row = (at + k) * SUB
            i = bisect.bisect_right(cuts, row) - 1
            outs[i][:, row - cuts[i] : row - cuts[i] + SUB, :] = y[:, k * width : (k + 1) * width].reshape(n, SUB, width)


def mix(given, pieces, cuts, back=False):
    n, _, width = pieces[0].shape
    part = cuts[-1]
    shapes = [jax.ShapeDtypeStruct((n, b - a, width), F32) for a, b in zip(cuts[:-1], cuts[1:])]
    if not back:
        shapes.append(jax.ShapeDtypeStruct((n, n), F32))
    return pl.pallas_call(
        functools.partial(mix_kernel, cuts, back),
        out_shape=shapes,
        in_specs=([FULL] if back else [SCALAR, FULL]) + [FULL] * len(pieces),
        out_specs=[FULL] * len(shapes),
        compiler_params=params(16),
        cost_estimate=pl.CostEstimate(
            flops=6 * n * n * part * width * SUB, bytes_accessed=8 * n * part * width, transcendentals=0
        ),
    )(*given, *pieces)


def gather_side(ref, rows_of, scratch_high, scratch_low):
    n, part, width = ref.shape
    n_z = scratch_high.shape[1] // width
    for g in range(n // n_z):
        span = slice(g * part, (g + 1) * part)
        live = g * part + lax.broadcasted_iota(jnp.int32, (part, width), 0) < rows_of
        for k in range(n_z):
            high, low = halves(jnp.where(live, ref[g * n_z + k], 0.0))
            scratch_high[span, k * width : (k + 1) * width] = high
            scratch_low[span, k * width : (k + 1) * width] = low


def own_kernel(scale, block, at, rows, side, inter, acc, lin_h, lin_l, v, raw, side_h, side_l, sem):
    height = v.shape[0]
    first = pltpu.make_async_copy(side, raw, sem.at[0])
    first.start()
    copies = [
        pltpu.make_async_copy(inter.at[at[0], pl.ds(r, block)], v.at[pl.ds(r, block)], sem.at[1 + r // block])
        for r in range(0, height, block)
    ]
    for copy in copies:
        copy.start()
    first.wait()
    gather_side(raw, rows[at[0]], side_h, side_l)
    mine = (side_h[...], side_l[...])
    for r, copy in zip(range(0, height, block), copies):
        copy.wait()
        linear = dot3(halves(v[r : r + block]), mine)
        acc[r : r + block] = linear
        lin_h[r : r + block], lin_l[r : r + block] = halves(linear)
    inner = halves(dot3(mine, (lin_h[...], lin_l[...]), ((0,), (0,))) * scale)
    for r in range(0, height, block):
        acc[r : r + block] += dot3(tuple(s[r : r + block] for s in mine), inner)


def own(at, rows, side, inter, scale, block=256):
    n, part, width = side.shape
    height = inter.shape[1]
    cols = n * part * width // height
    sds = jax.ShapeDtypeStruct
    return pl.pallas_call(
        functools.partial(own_kernel, scale, block),
        out_shape=[sds((height, cols), F32), sds((height, cols), BF16), sds((height, cols), BF16)],
        in_specs=[SCALAR, SCALAR, ANY, ANY],
        out_specs=[FULL] * 3,
        scratch_shapes=[
            pltpu.VMEM((height, height), F32),
            pltpu.VMEM(side.shape, F32),
            pltpu.VMEM((height, cols), BF16),
            pltpu.VMEM((height, cols), BF16),
            pltpu.SemaphoreType.DMA((1 + height // block,)),
        ],
        compiler_params=params(OWN_MIB),
        cost_estimate=pl.CostEstimate(
            flops=12 * height * height * cols, bytes_accessed=4 * height * (height + 3 * cols), transcendentals=0
        ),
    )(at, rows, side, inter)


def other_kernel(scale, cuts, at, rows, side, base, lin_h, lin_l, *refs):
    outs, (side_h, side_l) = refs[:-2], refs[-2:]
    n, part, width = side.shape
    n_z = side_h.shape[1] // width
    gather_side(side, rows[at[0]], side_h, side_l)
    theirs = (side_h[...], side_l[...])
    inner = halves(dot3(theirs, (lin_h[...], lin_l[...]), ((0,), (0,))) * scale)
    step = 4
    for g0 in range(0, n // n_z, step):
        span = slice(g0 * part, (g0 + step) * part)
        total = base[span] + dot3(tuple(s[span] for s in theirs), inner)
        live = g0 * part + lax.broadcasted_iota(jnp.int32, total.shape, 0) < rows[at[0]]
        total = jnp.where(live, total, 0.0)
        for g in range(step):
            for k in range(n_z):
                tile = total[g * part : (g + 1) * part, k * width : (k + 1) * width]
                for i, out in enumerate(outs):
                    out[(g0 + g) * n_z + k] = tile[cuts[i] : cuts[i + 1]]


def other(at, rows, side, base, lin_h, lin_l, scale, cuts):
    n, part, width = side.shape
    height, cols = base.shape
    return pl.pallas_call(
        functools.partial(other_kernel, scale, cuts),
        out_shape=[jax.ShapeDtypeStruct((n, b - a, width), F32) for a, b in zip(cuts[:-1], cuts[1:])],
        in_specs=[SCALAR, SCALAR] + [FULL] * 4,
        out_specs=[FULL] * (len(cuts) - 1),
        scratch_shapes=[pltpu.VMEM((height, cols), BF16)] * 2,
        compiler_params=params(24),
        cost_estimate=pl.CostEstimate(
            flops=12 * height * cols * cols, bytes_accessed=16 * height * cols, transcendentals=0
        ),
    )(at, rows, side, base, lin_h, lin_l)


def finish_kernel(cuts, below, *refs):
    ins, out = refs[:-1], refs[-1]
    for i, ref in enumerate(ins):
        rows = slice(cuts[i], cuts[i + 1])
        out[0, :, rows] = ref[:, 0] / below[0, :, rows]


def finish(pieces, below, n, cuts):
    c, height, width = below.shape
    part = height // n
    whole = pl.BlockSpec((1, n, part, width), lambda i: (i, 0, 0, 0))
    sizes = [b - a for a, b in zip(cuts[:-1], cuts[1:])]
    return pl.pallas_call(
        functools.partial(finish_kernel, cuts),
        grid=(c,),
        out_shape=jax.ShapeDtypeStruct((c, n, part, width), F32),
        in_specs=[whole] + [pl.BlockSpec((n, 1, rows, width), lambda i: (0, i, 0, 0)) for rows in sizes],
        out_specs=whole,
        compiler_params=params(12),
        cost_estimate=pl.CostEstimate(flops=c * height * width, bytes_accessed=12 * c * height * width, transcendentals=0),
    )(below.reshape(c, n, part, width), *[p.reshape(n, c, rows, width) for p, rows in zip(pieces, sizes)]).reshape(c, height, width)


def exchange(pieces, axes):
    return [lax.all_to_all(piece, axes, split_axis=0, concat_axis=0, tiled=True) for piece in pieces]


def per_device(amplitudes, interaction, sixj_values, sixj_index, ph_rows, denominators):
    c, height, width = amplitudes.shape
    n_chan, n_z = lax.axis_size("chan"), lax.axis_size("z")
    z, core = lax.axis_index("z"), lax.axis_index("core")
    at = jnp.reshape(z, (1,)).astype(jnp.int32)
    scale = 1.0 / (height * width * n_z * 2) ** 0.5

    def forward(core):
        def run(blocks, *given):
            parts = exchange(deal(blocks, n_chan, FIRST[core]), "chan")
            mixed, table = mix(given, parts, (0, height // n_chan))
            return exchange([mixed], CHIPS)[0], table

        return run

    def backward(core):
        def run(at, rows, theirs, table, below, *sums):
            cycle = other(at, rows, theirs, *sums, scale, THIRD[core])
            back = mix((table,), exchange(cycle, CHIPS), LAST[core], back=True)
            return finish(exchange(back, "chan"), below, n_chan, LAST[core])

        return run

    mine, table = lax.cond(core == 0, forward(0), forward(1), amplitudes, sixj_values, sixj_index)
    theirs = lax.ppermute(mine, "core", [(0, 1), (1, 0)])
    sums = own(at, ph_rows, mine, interaction, scale)
    return lax.cond(core == 0, backward(0), backward(1), at, ph_rows, theirs, table, denominators, *sums)


def solution(mesh):
    split = Mesh(mesh.devices.reshape(mesh.devices.shape[0], -1, 2), ("chan", "z", "core"))
    hole = ("z", "core")
    in_specs = (
        P("chan", None, hole),
        P("chan", None, None),
        P(),
        P(),
        P("chan"),
        P("chan", None, hole),
    )
    return jax.shard_map(
        per_device, mesh=split, in_specs=in_specs, out_specs=P("chan", None, hole), check_vma=False
    )
```

```python
import bisect
import functools
import jax
import jax.numpy as jnp
from jax import lax
from jax.experimental import pallas as pl
from jax.experimental.pallas import tpu as pltpu
from jax.sharding import Mesh, PartitionSpec as P

CHIPS = ("chan", "z")
FIRST = ((0, 64), (0, 8, 64))
THIRD = ((0, 64), (0, 8, 64))
LAST = ((0, 64), (0, 64))
MIB = 2**20
BF16, F32 = jnp.bfloat16, jnp.float32
ANY = pl.BlockSpec(memory_space=pl.ANY)
FULL = pl.BlockSpec(memory_space=pltpu.VMEM)
SCALAR = pl.BlockSpec(memory_space=pltpu.SMEM)
SUB = 8


def halves(x):
    high = x.astype(BF16)
    return high, (x - high.astype(F32)).astype(BF16)


def dot3(a, b, dims=((1,), (0,))):
    def one(x, y):
        return lax.dot_general(x, y, (dims, ((), ())), preferred_element_type=F32)

    return one(a[0], b[0]) + (one(a[0], b[1]) + one(a[1], b[0]))


def params(mib):
    return pltpu.CompilerParams(vmem_limit_bytes=mib * MIB)


def deal_kernel(cuts, blocks, *refs):
    outs, sems = refs[:-1], refs[-1]
    copies = [
        pltpu.make_async_copy(
            blocks.at[c, :, pl.ds(cuts[k], cuts[k + 1] - cuts[k])], out.at[:, c], sems.at[k * blocks.shape[0] + c]
        )
        for k, out in enumerate(outs)
        for c in range(blocks.shape[0])
    ]
    for copy in copies:
        copy.start()
    for copy in copies:
        copy.wait()


def deal(blocks, n, cuts):
    c, height, width = blocks.shape
    part = height // n
    sizes = [b - a for a, b in zip(cuts[:-1], cuts[1:])]
    pieces = pl.pallas_call(
        functools.partial(deal_kernel, cuts),
        out_shape=[jax.ShapeDtypeStruct((n, c, rows, width), F32) for rows in sizes],
        in_specs=[ANY],
        out_specs=[FULL] * len(sizes),
        scratch_shapes=[pltpu.SemaphoreType.DMA((len(sizes) * c,))],
        compiler_params=params(8),
        cost_estimate=pl.CostEstimate(flops=0, bytes_accessed=8 * c * height * width, transcendentals=0),
    )(blocks.reshape(c, n, part, width))
    return [piece.reshape(n * c, rows, width) for piece, rows in zip(pieces, sizes)]


def spread_table(table):
    n = table.shape[0]
    wide = n * SUB
    rows = (lax.broadcasted_iota(jnp.int32, (wide, n), 0) // SUB == lax.broadcasted_iota(jnp.int32, (wide, n), 1)).astype(BF16)
    columns = (lax.broadcasted_iota(jnp.int32, (n, wide), 1) // SUB == lax.broadcasted_iota(jnp.int32, (n, wide), 0)).astype(BF16)
    same = lax.broadcasted_iota(jnp.int32, (wide, wide), 0) % SUB == lax.broadcasted_iota(jnp.int32, (wide, wide), 1) % SUB
    spread = []
    for part in halves(table):
        tall = jnp.dot(rows, part, preferred_element_type=F32).astype(BF16)
        both = jnp.dot(tall, columns, preferred_element_type=F32)
        spread.append(jnp.where(same, both, 0.0).astype(BF16))
    return tuple(spread)


def mix_kernel(cuts, back, *refs):
    n_in, n_out = (1, len(cuts) - 1) if back else (2, len(cuts))
    given, pieces, outs = refs[:n_in], refs[n_in:-n_out], refs[-n_out:]
    n, _, width = outs[0].shape
    if back:
        table = given[0][...].T
    else:
        values, index = given
        table = jnp.zeros(index.shape, F32)
        for slot in range(values.shape[0]):
            table = jnp.where(index[...] == slot, values[slot], table)
        outs[-1][...] = table
    spread = spread_table(table)
    groups = [(ref, row) for ref in pieces for row in range(0, ref.shape[1], SUB)]
    for at in range(0, len(groups), 2):
        x = jnp.concatenate(
            [ref[:, row : row + SUB, :].reshape(n * SUB, width) for ref, row in groups[at : at + 2]], axis=1
        )
        y = dot3(spread, halves(x))
        for k in range(2):
            row = (at + k) * SUB
            i = bisect.bisect_right(cuts, row) - 1
            outs[i][:, row - cuts[i] : row - cuts[i] + SUB, :] = y[:, k * width : (k + 1) * width].reshape(n, SUB, width)


def mix(given, pieces, cuts, back=False):
    n, _, width = pieces[0].shape
    part = cuts[-1]
    shapes = [jax.ShapeDtypeStruct((n, b - a, width), F32) for a, b in zip(cuts[:-1], cuts[1:])]
    if not back:
        shapes.append(jax.ShapeDtypeStruct((n, n), F32))
    return pl.pallas_call(
        functools.partial(mix_kernel, cuts, back),
        out_shape=shapes,
        in_specs=([FULL] if back else [SCALAR, FULL]) + [FULL] * len(pieces),
        out_specs=[FULL] * len(shapes),
        compiler_params=params(16),
        cost_estimate=pl.CostEstimate(
            flops=6 * n * n * part * width * SUB, bytes_accessed=8 * n * part * width, transcendentals=0
        ),
    )(*given, *pieces)


def gather_side(ref, rows_of, scratch_high, scratch_low):
    n, part, width = ref.shape
    n_z = scratch_high.shape[1] // width
    for g in range(n // n_z):
        span = slice(g * part, (g + 1) * part)
        live = g * part + lax.broadcasted_iota(jnp.int32, (part, width), 0) < rows_of
        for k in range(n_z):
            high, low = halves(jnp.where(live, ref[g * n_z + k], 0.0))
            scratch_high[span, k * width : (k + 1) * width] = high
            scratch_low[span, k * width : (k + 1) * width] = low


def own_kernel(scale, block, at, rows, side, inter, acc, lin_h, lin_l, v, side_h, side_l, sem):
    height = v.shape[0]
    copies = [
        pltpu.make_async_copy(inter.at[at[0], pl.ds(r, block)], v.at[pl.ds(r, block)], sem.at[r // block])
        for r in range(0, height, block)
    ]
    for copy in copies:
        copy.start()
    gather_side(side, rows[at[0]], side_h, side_l)
    mine = (side_h[...], side_l[...])
    for r, copy in zip(range(0, height, block), copies):
        copy.wait()
        linear = dot3(halves(v[r : r + block]), mine)
        acc[r : r + block] = linear
        lin_h[r : r + block], lin_l[r : r + block] = halves(linear)
    inner = halves(dot3(mine, (lin_h[...], lin_l[...]), ((0,), (0,))) * scale)
    for r in range(0, height, block):
        acc[r : r + block] += dot3(tuple(s[r : r + block] for s in mine), inner)


def own(at, rows, side, inter, scale, block=256):
    n, part, width = side.shape
    height = inter.shape[1]
    cols = n * part * width // height
    sds = jax.ShapeDtypeStruct
    return pl.pallas_call(
        functools.partial(own_kernel, scale, block),
        out_shape=[sds((height, cols), F32), sds((height, cols), BF16), sds((height, cols), BF16)],
        in_specs=[SCALAR, SCALAR, FULL, ANY],
        out_specs=[FULL] * 3,
        scratch_shapes=[
            pltpu.VMEM((height, height), F32),
            pltpu.VMEM((height, cols), BF16),
            pltpu.VMEM((height, cols), BF16),
            pltpu.SemaphoreType.DMA((height // block,)),
        ],
        compiler_params=params(24),
        cost_estimate=pl.CostEstimate(
            flops=12 * height * height * cols, bytes_accessed=4 * height * (height + 3 * cols), transcendentals=0
        ),
    )(
        at,
        rows,
        pltpu.with_memory_space_constraint(side, pltpu.VMEM),
        pltpu.with_memory_space_constraint(inter, pltpu.HBM),
    )


def other_kernel(scale, cuts, at, rows, side, base, lin_h, lin_l, *refs):
    outs, (side_h, side_l) = refs[:-2], refs[-2:]
    n, part, width = side.shape
    n_z = side_h.shape[1] // width
    gather_side(side, rows[at[0]], side_h, side_l)
    theirs = (side_h[...], side_l[...])
    inner = halves(dot3(theirs, (lin_h[...], lin_l[...]), ((0,), (0,))) * scale)
    step = 4
    for g0 in range(0, n // n_z, step):
        span = slice(g0 * part, (g0 + step) * part)
        total = base[span] + dot3(tuple(s[span] for s in theirs), inner)
        live = g0 * part + lax.broadcasted_iota(jnp.int32, total.shape, 0) < rows[at[0]]
        total = jnp.where(live, total, 0.0)
        for g in range(step):
            for k in range(n_z):
                tile = total[g * part : (g + 1) * part, k * width : (k + 1) * width]
                for i, out in enumerate(outs):
                    out[(g0 + g) * n_z + k] = tile[cuts[i] : cuts[i + 1]]


def other(at, rows, side, base, lin_h, lin_l, scale, cuts):
    n, part, width = side.shape
    height, cols = base.shape
    return pl.pallas_call(
        functools.partial(other_kernel, scale, cuts),
        out_shape=[jax.ShapeDtypeStruct((n, b - a, width), F32) for a, b in zip(cuts[:-1], cuts[1:])],
        in_specs=[SCALAR, SCALAR] + [FULL] * 4,
        out_specs=[FULL] * (len(cuts) - 1),
        scratch_shapes=[pltpu.VMEM((height, cols), BF16)] * 2,
        compiler_params=params(24),
        cost_estimate=pl.CostEstimate(
            flops=12 * height * cols * cols, bytes_accessed=16 * height * cols, transcendentals=0
        ),
    )(at, rows, pltpu.with_memory_space_constraint(side, pltpu.VMEM), base, lin_h, lin_l)


def finish_kernel(cuts, below, *refs):
    ins, out = refs[:-1], refs[-1]
    for i, ref in enumerate(ins):
        rows = slice(cuts[i], cuts[i + 1])
        out[0, :, rows] = ref[:, 0] / below[0, :, rows]


def finish(pieces, below, n, cuts):
    c, height, width = below.shape
    part = height // n
    whole = pl.BlockSpec((1, n, part, width), lambda i: (i, 0, 0, 0))
    sizes = [b - a for a, b in zip(cuts[:-1], cuts[1:])]
    return pl.pallas_call(
        functools.partial(finish_kernel, cuts),
        grid=(c,),
        out_shape=jax.ShapeDtypeStruct((c, n, part, width), F32),
        in_specs=[whole] + [pl.BlockSpec((n, 1, rows, width), lambda i: (0, i, 0, 0)) for rows in sizes],
        out_specs=whole,
        compiler_params=params(12),
        cost_estimate=pl.CostEstimate(flops=c * height * width, bytes_accessed=12 * c * height * width, transcendentals=0),
    )(below.reshape(c, n, part, width), *[p.reshape(n, c, rows, width) for p, rows in zip(pieces, sizes)]).reshape(c, height, width)


def exchange(pieces, axes):
    return [lax.all_to_all(piece, axes, split_axis=0, concat_axis=0, tiled=True) for piece in pieces]


def per_device(amplitudes, interaction, sixj_values, sixj_index, ph_rows, denominators):
    c, height, width = amplitudes.shape
    n_chan, n_z = lax.axis_size("chan"), lax.axis_size("z")
    z, core = lax.axis_index("z"), lax.axis_index("core")
    at = jnp.reshape(z, (1,)).astype(jnp.int32)
    scale = 1.0 / (height * width * n_z * 2) ** 0.5

    def forward(core):
        def run(blocks, *given):
            parts = exchange(deal(blocks, n_chan, FIRST[core]), "chan")
            mixed, table = mix(given, parts, (0, height // n_chan))
            return exchange([mixed], CHIPS)[0], table

        return run

    def backward(core):
        def run(at, rows, theirs, table, below, *sums):
            cycle = other(at, rows, theirs, *sums, scale, THIRD[core])
            back = mix((table,), exchange(cycle, CHIPS), LAST[core], back=True)
            return finish(exchange(back, "chan"), below, n_chan, LAST[core])

        return run

    mine, table = lax.cond(core == 0, forward(0), forward(1), amplitudes, sixj_values, sixj_index)
    theirs = lax.ppermute(mine, "core", [(0, 1), (1, 0)])
    sums = own(at, ph_rows, mine, interaction, scale)
    return lax.cond(core == 0, backward(0), backward(1), at, ph_rows, theirs, table, denominators, *sums)


def solution(mesh):
    split = Mesh(mesh.devices.reshape(mesh.devices.shape[0], -1, 2), ("chan", "z", "core"))
    hole = ("z", "core")
    in_specs = (
        P("chan", None, hole),
        P("chan", None, None),
        P(),
        P(),
        P("chan"),
        P("chan", None, hole),
    )
    return jax.shard_map(
        per_device, mesh=split, in_specs=in_specs, out_specs=P("chan", None, hole), check_vma=False
    )
```

```python
import bisect
import functools
import jax
import jax.numpy as jnp
from jax import lax
from jax.experimental import pallas as pl
from jax.experimental.pallas import tpu as pltpu
from jax.sharding import Mesh, PartitionSpec as P

CHIPS = ("chan", "z")
FIRST = ((0, 64), (0, 8, 64))
THIRD = ((0, 64), (0, 8, 64))
LAST = ((0, 64), (0, 64))
MIB = 2**20
BF16, F32 = jnp.bfloat16, jnp.float32
ANY = pl.BlockSpec(memory_space=pl.ANY)
FULL = pl.BlockSpec(memory_space=pltpu.VMEM)
SCALAR = pl.BlockSpec(memory_space=pltpu.SMEM)
SUB = 8


def halves(x):
    high = x.astype(BF16)
    return high, (x - high.astype(F32)).astype(BF16)


def dot3(a, b, dims=((1,), (0,))):
    def one(x, y):
        return lax.dot_general(x, y, (dims, ((), ())), preferred_element_type=F32)

    return one(a[0], b[0]) + (one(a[0], b[1]) + one(a[1], b[0]))


def params(mib):
    return pltpu.CompilerParams(vmem_limit_bytes=mib * MIB)


def spread_table(table):
    n = table.shape[0]
    wide = n * SUB
    rows = (lax.broadcasted_iota(jnp.int32, (wide, n), 0) // SUB == lax.broadcasted_iota(jnp.int32, (wide, n), 1)).astype(BF16)
    columns = (lax.broadcasted_iota(jnp.int32, (n, wide), 1) // SUB == lax.broadcasted_iota(jnp.int32, (n, wide), 0)).astype(BF16)
    same = lax.broadcasted_iota(jnp.int32, (wide, wide), 0) % SUB == lax.broadcasted_iota(jnp.int32, (wide, wide), 1) % SUB
    spread = []
    for part in halves(table):
        tall = jnp.dot(rows, part, preferred_element_type=F32).astype(BF16)
        both = jnp.dot(tall, columns, preferred_element_type=F32)
        spread.append(jnp.where(same, both, 0.0).astype(BF16))
    return tuple(spread)


def deal_kernel(cuts, blocks, values, index, *refs):
    n_out = len(cuts) - 1
    outs, (table, spread_h, spread_l, slots, known, sems) = refs[:n_out], refs[n_out:]
    c = blocks.shape[0]
    copies = [
        pltpu.make_async_copy(blocks.at[i, :, pl.ds(cuts[k], cuts[k + 1] - cuts[k])], out.at[:, i], sems.at[k * c + i])
        for k, out in enumerate(outs)
        for i in range(c)
    ]
    small = [
        pltpu.make_async_copy(index, slots, sems.at[n_out * c]),
        pltpu.make_async_copy(values, known, sems.at[n_out * c + 1]),
    ]
    for copy in small + copies:
        copy.start()
    for copy in small:
        copy.wait()
    made = jnp.zeros(index.shape, F32)
    for slot in range(values.shape[0]):
        made = jnp.where(slots[...] == slot, known[slot], made)
    table[...] = made
    spread_h[...], spread_l[...] = spread_table(made)
    for copy in copies:
        copy.wait()


def deal(blocks, values, index, n, cuts):
    c, height, width = blocks.shape
    part = height // n
    sizes = [b - a for a, b in zip(cuts[:-1], cuts[1:])]
    wide = index.shape[0] * SUB
    sds = jax.ShapeDtypeStruct
    *pieces, table, spread_h, spread_l = pl.pallas_call(
        functools.partial(deal_kernel, cuts),
        out_shape=[sds((n, c, rows, width), F32) for rows in sizes]
        + [sds(index.shape, F32), sds((wide, wide), BF16), sds((wide, wide), BF16)],
        in_specs=[ANY] * 3,
        out_specs=[FULL] * (len(sizes) + 3),
        scratch_shapes=[
            pltpu.VMEM(index.shape, jnp.int32),
            pltpu.SMEM(values.shape, F32),
            pltpu.SemaphoreType.DMA((len(sizes) * c + 2,)),
        ],
        compiler_params=params(12),
        cost_estimate=pl.CostEstimate(flops=0, bytes_accessed=8 * c * height * width, transcendentals=0),
    )(blocks.reshape(c, n, part, width), values, index)
    return [piece.reshape(n * c, rows, width) for piece, rows in zip(pieces, sizes)], table, (spread_h, spread_l)


def mix_kernel(cuts, n_in, *refs):
    n_out = len(cuts) - 1
    given, pieces, outs = refs[:n_in], refs[n_in:-n_out], refs[-n_out:]
    n, _, width = outs[0].shape
    spread = spread_table(given[0][...].T) if n_in == 1 else tuple(ref[...] for ref in given)
    groups = [(ref, row) for ref in pieces for row in range(0, ref.shape[1], SUB)]
    for at in range(0, len(groups), 2):
        x = jnp.concatenate(
            [ref[:, row : row + SUB, :].reshape(n * SUB, width) for ref, row in groups[at : at + 2]], axis=1
        )
        y = dot3(spread, halves(x))
        for k in range(2):
            row = (at + k) * SUB
            i = bisect.bisect_right(cuts, row) - 1
            outs[i][:, row - cuts[i] : row - cuts[i] + SUB, :] = y[:, k * width : (k + 1) * width].reshape(n, SUB, width)


def mix(given, pieces, cuts):
    n, _, width = pieces[0].shape
    part = cuts[-1]
    return pl.pallas_call(
        functools.partial(mix_kernel, cuts, len(given)),
        out_shape=[jax.ShapeDtypeStruct((n, b - a, width), F32) for a, b in zip(cuts[:-1], cuts[1:])],
        in_specs=[FULL] * (len(given) + len(pieces)),
        out_specs=[FULL] * (len(cuts) - 1),
        compiler_params=params(16),
        cost_estimate=pl.CostEstimate(
            flops=6 * n * n * part * width * SUB, bytes_accessed=8 * n * part * width, transcendentals=0
        ),
    )(*given, *pieces)


def gather_side(ref, rows_of, scratch_high, scratch_low):
    n, part, width = ref.shape
    n_z = scratch_high.shape[1] // width
    for g in range(n // n_z):
        span = slice(g * part, (g + 1) * part)
        live = g * part + lax.broadcasted_iota(jnp.int32, (part, width), 0) < rows_of
        for k in range(n_z):
            high, low = halves(jnp.where(live, ref[g * n_z + k], 0.0))
            scratch_high[span, k * width : (k + 1) * width] = high
            scratch_low[span, k * width : (k + 1) * width] = low


def own_kernel(scale, block, at, rows, side, inter, acc, lin_h, lin_l, v, side_h, side_l, sem):
    height = v.shape[0]
    copies = [
        pltpu.make_async_copy(inter.at[at[0], pl.ds(r, block)], v.at[pl.ds(r, block)], sem.at[r // block])
        for r in range(0, height, block)
    ]
    for copy in copies:
        copy.start()
    gather_side(side, rows[at[0]], side_h, side_l)
    mine = (side_h[...], side_l[...])
    for r, copy in zip(range(0, height, block), copies):
        copy.wait()
        linear = dot3(halves(v[r : r + block]), mine)
        acc[r : r + block] = linear
        lin_h[r : r + block], lin_l[r : r + block] = halves(linear)
    inner = halves(dot3(mine, (lin_h[...], lin_l[...]), ((0,), (0,))) * scale)
    for r in range(0, height, block):
        acc[r : r + block] += dot3(tuple(s[r : r + block] for s in mine), inner)


def own(at, rows, side, inter, scale, block=256):
    n, part, width = side.shape
    height = inter.shape[1]
    cols = n * part * width // height
    sds = jax.ShapeDtypeStruct
    return pl.pallas_call(
        functools.partial(own_kernel, scale, block),
        out_shape=[sds((height, cols), F32), sds((height, cols), BF16), sds((height, cols), BF16)],
        in_specs=[SCALAR, SCALAR, FULL, ANY],
        out_specs=[FULL] * 3,
        scratch_shapes=[
            pltpu.VMEM((height, height), F32),
            pltpu.VMEM((height, cols), BF16),
            pltpu.VMEM((height, cols), BF16),
            pltpu.SemaphoreType.DMA((height // block,)),
        ],
        compiler_params=params(24),
        cost_estimate=pl.CostEstimate(
            flops=12 * height * height * cols, bytes_accessed=4 * height * (height + 3 * cols), transcendentals=0
        ),
    )(
        at,
        rows,
        pltpu.with_memory_space_constraint(side, pltpu.VMEM),
        pltpu.with_memory_space_constraint(inter, pltpu.HBM),
    )


def other_kernel(scale, cuts, at, rows, side, base, lin_h, lin_l, *refs):
    outs, (side_h, side_l) = refs[:-2], refs[-2:]
    n, part, width = side.shape
    n_z = side_h.shape[1] // width
    gather_side(side, rows[at[0]], side_h, side_l)
    theirs = (side_h[...], side_l[...])
    inner = halves(dot3(theirs, (lin_h[...], lin_l[...]), ((0,), (0,))) * scale)
    step = 4
    for g0 in range(0, n // n_z, step):
        span = slice(g0 * part, (g0 + step) * part)
        total = base[span] + dot3(tuple(s[span] for s in theirs), inner)
        live = g0 * part + lax.broadcasted_iota(jnp.int32, total.shape, 0) < rows[at[0]]
        total = jnp.where(live, total, 0.0)
        for g in range(step):
            for k in range(n_z):
                tile = total[g * part : (g + 1) * part, k * width : (k + 1) * width]
                for i, out in enumerate(outs):
                    out[(g0 + g) * n_z + k] = tile[cuts[i] : cuts[i + 1]]


def other(at, rows, side, base, lin_h, lin_l, scale, cuts):
    n, part, width = side.shape
    height, cols = base.shape
    return pl.pallas_call(
        functools.partial(other_kernel, scale, cuts),
        out_shape=[jax.ShapeDtypeStruct((n, b - a, width), F32) for a, b in zip(cuts[:-1], cuts[1:])],
        in_specs=[SCALAR, SCALAR] + [FULL] * 4,
        out_specs=[FULL] * (len(cuts) - 1),
        scratch_shapes=[pltpu.VMEM((height, cols), BF16)] * 2,
        compiler_params=params(24),
        cost_estimate=pl.CostEstimate(
            flops=12 * height * cols * cols, bytes_accessed=16 * height * cols, transcendentals=0
        ),
    )(at, rows, pltpu.with_memory_space_constraint(side, pltpu.VMEM), base, lin_h, lin_l)


def finish_kernel(cuts, below, *refs):
    ins, out = refs[:-1], refs[-1]
    for i, ref in enumerate(ins):
        rows = slice(cuts[i], cuts[i + 1])
        out[0, :, rows] = ref[:, 0] / below[0, :, rows]


def finish(pieces, below, n, cuts):
    c, height, width = below.shape
    part = height // n
    whole = pl.BlockSpec((1, n, part, width), lambda i: (i, 0, 0, 0))
    sizes = [b - a for a, b in zip(cuts[:-1], cuts[1:])]
    return pl.pallas_call(
        functools.partial(finish_kernel, cuts),
        grid=(c,),
        out_shape=jax.ShapeDtypeStruct((c, n, part, width), F32),
        in_specs=[whole] + [pl.BlockSpec((n, 1, rows, width), lambda i: (0, i, 0, 0)) for rows in sizes],
        out_specs=whole,
        compiler_params=params(12),
        cost_estimate=pl.CostEstimate(flops=c * height * width, bytes_accessed=12 * c * height * width, transcendentals=0),
    )(below.reshape(c, n, part, width), *[p.reshape(n, c, rows, width) for p, rows in zip(pieces, sizes)]).reshape(c, height, width)


def exchange(pieces, axes):
    return [lax.all_to_all(piece, axes, split_axis=0, concat_axis=0, tiled=True) for piece in pieces]


def per_device(amplitudes, interaction, sixj_values, sixj_index, ph_rows, denominators):
    c, height, width = amplitudes.shape
    n_chan, n_z = lax.axis_size("chan"), lax.axis_size("z")
    z, core = lax.axis_index("z"), lax.axis_index("core")
    at = jnp.reshape(z, (1,)).astype(jnp.int32)
    scale = 1.0 / (height * width * n_z * 2) ** 0.5

    def forward(core):
        def run(blocks, values, index):
            pieces, table, spread = deal(blocks, values, index, n_chan, FIRST[core])
            mixed = mix(spread, exchange(pieces, "chan"), (0, height // n_chan))
            return exchange(mixed, CHIPS)[0], table

        return run

    def backward(core):
        def run(at, rows, theirs, table, below, *sums):
            cycle = other(at, rows, theirs, *sums, scale, THIRD[core])
            back = mix((table,), exchange(cycle, CHIPS), LAST[core])
            return finish(exchange(back, "chan"), below, n_chan, LAST[core])

        return run

    mine, table = lax.cond(core == 0, forward(0), forward(1), amplitudes, sixj_values, sixj_index)
    theirs = lax.ppermute(mine, "core", [(0, 1), (1, 0)])
    sums = own(at, ph_rows, mine, interaction, scale)
    return lax.cond(core == 0, backward(0), backward(1), at, ph_rows, theirs, table, denominators, *sums)


def solution(mesh):
    split = Mesh(mesh.devices.reshape(mesh.devices.shape[0], -1, 2), ("chan", "z", "core"))
    hole = ("z", "core")
    in_specs = (
        P("chan", None, hole),
        P("chan", None, None),
        P(),
        P(),
        P("chan"),
        P("chan", None, hole),
    )
    return jax.shard_map(
        per_device, mesh=split, in_specs=in_specs, out_specs=P("chan", None, hole), check_vma=False
    )
```

```python
import bisect
import functools
import jax
import jax.numpy as jnp
from jax import lax
from jax.experimental import pallas as pl
from jax.experimental.pallas import tpu as pltpu
from jax.sharding import Mesh, PartitionSpec as P

CHIPS = ("chan", "z")
FIRST = ((0, 64), (0, 16, 64))
THIRD = ((0, 64), (0, 8, 64))
LAST = ((0, 64), (0, 64))
MIB = 2**20
BF16, F32 = jnp.bfloat16, jnp.float32
ANY = pl.BlockSpec(memory_space=pl.ANY)
FULL = pl.BlockSpec(memory_space=pltpu.VMEM)
SCALAR = pl.BlockSpec(memory_space=pltpu.SMEM)
SUB = 8


def halves(x):
    high = x.astype(BF16)
    return high, (x - high.astype(F32)).astype(BF16)


def dot3(a, b, dims=((1,), (0,))):
    def one(x, y):
        return lax.dot_general(x, y, (dims, ((), ())), preferred_element_type=F32)

    return one(a[0], b[0]) + (one(a[0], b[1]) + one(a[1], b[0]))


def params(mib):
    return pltpu.CompilerParams(vmem_limit_bytes=mib * MIB)


def spread_table(table):
    n = table.shape[0]
    wide = n * SUB
    rows = (lax.broadcasted_iota(jnp.int32, (wide, n), 0) // SUB == lax.broadcasted_iota(jnp.int32, (wide, n), 1)).astype(BF16)
    columns = (lax.broadcasted_iota(jnp.int32, (n, wide), 1) // SUB == lax.broadcasted_iota(jnp.int32, (n, wide), 0)).astype(BF16)
    same = lax.broadcasted_iota(jnp.int32, (wide, wide), 0) % SUB == lax.broadcasted_iota(jnp.int32, (wide, wide), 1) % SUB
    spread = []
    for part in halves(table):
        tall = jnp.dot(rows, part, preferred_element_type=F32).astype(BF16)
        both = jnp.dot(tall, columns, preferred_element_type=F32)
        spread.append(jnp.where(same, both, 0.0).astype(BF16))
    return tuple(spread)


def deal_kernel(cuts, blocks, values, index, *refs):
    n_out = len(cuts) - 1
    outs, (table, spread_h, spread_l, slots, known, sems) = refs[:n_out], refs[n_out:]
    c = blocks.shape[0]
    copies = [
        pltpu.make_async_copy(blocks.at[i, :, pl.ds(cuts[k], cuts[k + 1] - cuts[k])], out.at[:, i], sems.at[k * c + i])
        for k, out in enumerate(outs)
        for i in range(c)
    ]
    small = [
        pltpu.make_async_copy(index, slots, sems.at[n_out * c]),
        pltpu.make_async_copy(values, known, sems.at[n_out * c + 1]),
    ]
    for copy in small + copies:
        copy.start()
    for copy in small:
        copy.wait()
    made = jnp.zeros(index.shape, F32)
    for slot in range(values.shape[0]):
        made = jnp.where(slots[...] == slot, known[slot], made)
    table[...] = made
    spread_h[...], spread_l[...] = spread_table(made)
    for copy in copies:
        copy.wait()


def deal(blocks, values, index, n, cuts):
    c, height, width = blocks.shape
    part = height // n
    sizes = [b - a for a, b in zip(cuts[:-1], cuts[1:])]
    wide = index.shape[0] * SUB
    sds = jax.ShapeDtypeStruct
    *pieces, table, spread_h, spread_l = pl.pallas_call(
        functools.partial(deal_kernel, cuts),
        out_shape=[sds((n, c, rows, width), F32) for rows in sizes]
        + [sds(index.shape, F32), sds((wide, wide), BF16), sds((wide, wide), BF16)],
        in_specs=[ANY] * 3,
        out_specs=[FULL] * (len(sizes) + 3),
        scratch_shapes=[
            pltpu.VMEM(index.shape, jnp.int32),
            pltpu.SMEM(values.shape, F32),
            pltpu.SemaphoreType.DMA((len(sizes) * c + 2,)),
        ],
        compiler_params=params(12),
        cost_estimate=pl.CostEstimate(flops=0, bytes_accessed=8 * c * height * width, transcendentals=0),
    )(blocks.reshape(c, n, part, width), values, index)
    return [piece.reshape(n * c, rows, width) for piece, rows in zip(pieces, sizes)], table, (spread_h, spread_l)


def mix_kernel(cuts, n_in, *refs):
    n_out = len(cuts) - 1
    given, pieces, outs = refs[:n_in], refs[n_in:-n_out], refs[-n_out:]
    n, _, width = outs[0].shape
    spread = spread_table(given[0][...].T) if n_in == 1 else tuple(ref[...] for ref in given)
    groups = [(ref, row) for ref in pieces for row in range(0, ref.shape[1], SUB)]
    for at in range(0, len(groups), 2):
        x = jnp.concatenate(
            [ref[:, row : row + SUB, :].reshape(n * SUB, width) for ref, row in groups[at : at + 2]], axis=1
        )
        y = dot3(spread, halves(x))
        for k in range(2):
            row = (at + k) * SUB
            i = bisect.bisect_right(cuts, row) - 1
            outs[i][:, row - cuts[i] : row - cuts[i] + SUB, :] = y[:, k * width : (k + 1) * width].reshape(n, SUB, width)


def mix(given, pieces, cuts):
    n, _, width = pieces[0].shape
    part = cuts[-1]
    return pl.pallas_call(
        functools.partial(mix_kernel, cuts, len(given)),
        out_shape=[jax.ShapeDtypeStruct((n, b - a, width), F32) for a, b in zip(cuts[:-1], cuts[1:])],
        in_specs=[FULL] * (len(given) + len(pieces)),
        out_specs=[FULL] * (len(cuts) - 1),
        compiler_params=params(16),
        cost_estimate=pl.CostEstimate(
            flops=6 * n * n * part * width * SUB, bytes_accessed=8 * n * part * width, transcendentals=0
        ),
    )(*given, *pieces)


def gather_side(ref, rows_of, scratch_high, scratch_low):
    n, part, width = ref.shape
    n_z = scratch_high.shape[1] // width
    for g in range(n // n_z):
        span = slice(g * part, (g + 1) * part)
        live = g * part + lax.broadcasted_iota(jnp.int32, (part, width), 0) < rows_of
        for k in range(n_z):
            high, low = halves(jnp.where(live, ref[g * n_z + k], 0.0))
            scratch_high[span, k * width : (k + 1) * width] = high
            scratch_low[span, k * width : (k + 1) * width] = low


def own_kernel(scale, block, at, rows, side, inter, acc, lin_h, lin_l, v, side_h, side_l, sem):
    height = v.shape[0]
    copies = [
        pltpu.make_async_copy(inter.at[at[0], pl.ds(r, block)], v.at[pl.ds(r, block)], sem.at[r // block])
        for r in range(0, height, block)
    ]
    for copy in copies:
        copy.start()
    gather_side(side, rows[at[0]], side_h, side_l)
    mine = (side_h[...], side_l[...])
    for r, copy in zip(range(0, height, block), copies):
        copy.wait()
        linear = dot3(halves(v[r : r + block]), mine)
        acc[r : r + block] = linear
        lin_h[r : r + block], lin_l[r : r + block] = halves(linear)
    inner = halves(dot3(mine, (lin_h[...], lin_l[...]), ((0,), (0,))) * scale)
    for r in range(0, height, block):
        acc[r : r + block] += dot3(tuple(s[r : r + block] for s in mine), inner)


def own(at, rows, side, inter, scale, block=256):
    n, part, width = side.shape
    height = inter.shape[1]
    cols = n * part * width // height
    sds = jax.ShapeDtypeStruct
    return pl.pallas_call(
        functools.partial(own_kernel, scale, block),
        out_shape=[sds((height, cols), F32), sds((height, cols), BF16), sds((height, cols), BF16)],
        in_specs=[SCALAR, SCALAR, FULL, ANY],
        out_specs=[FULL] * 3,
        scratch_shapes=[
            pltpu.VMEM((height, height), F32),
            pltpu.VMEM((height, cols), BF16),
            pltpu.VMEM((height, cols), BF16),
            pltpu.SemaphoreType.DMA((height // block,)),
        ],
        compiler_params=params(24),
        cost_estimate=pl.CostEstimate(
            flops=12 * height * height * cols, bytes_accessed=4 * height * (height + 3 * cols), transcendentals=0
        ),
    )(
        at,
        rows,
        pltpu.with_memory_space_constraint(side, pltpu.VMEM),
        pltpu.with_memory_space_constraint(inter, pltpu.HBM),
    )


def other_kernel(scale, cuts, at, rows, table, side, base, lin_h, lin_l, *refs):
    outs, spreads, (raw, side_h, side_l, sem) = refs[:-6], refs[-6:-4], refs[-4:]
    arriving = pltpu.make_async_copy(side, raw, sem.at[0])
    arriving.start()
    for ref, value in zip(spreads, spread_table(table[...].T)):
        ref[...] = value
    arriving.wait()
    n, part, width = side.shape
    n_z = side_h.shape[1] // width
    gather_side(raw, rows[at[0]], side_h, side_l)
    theirs = (side_h[...], side_l[...])
    inner = halves(dot3(theirs, (lin_h[...], lin_l[...]), ((0,), (0,))) * scale)
    step = 4
    for g0 in range(0, n // n_z, step):
        span = slice(g0 * part, (g0 + step) * part)
        total = base[span] + dot3(tuple(s[span] for s in theirs), inner)
        live = g0 * part + lax.broadcasted_iota(jnp.int32, total.shape, 0) < rows[at[0]]
        total = jnp.where(live, total, 0.0)
        for g in range(step):
            for k in range(n_z):
                tile = total[g * part : (g + 1) * part, k * width : (k + 1) * width]
                for i, out in enumerate(outs):
                    out[(g0 + g) * n_z + k] = tile[cuts[i] : cuts[i + 1]]


def other(at, rows, table, side, base, lin_h, lin_l, scale, cuts):
    n, part, width = side.shape
    height, cols = base.shape
    wide = table.shape[0] * SUB
    *pieces, spread_h, spread_l = pl.pallas_call(
        functools.partial(other_kernel, scale, cuts),
        out_shape=[jax.ShapeDtypeStruct((n, b - a, width), F32) for a, b in zip(cuts[:-1], cuts[1:])]
        + [jax.ShapeDtypeStruct((wide, wide), BF16)] * 2,
        in_specs=[SCALAR, SCALAR, FULL, ANY] + [FULL] * 3,
        out_specs=[FULL] * (len(cuts) + 1),
        scratch_shapes=[pltpu.VMEM(side.shape, F32)]
        + [pltpu.VMEM((height, cols), BF16)] * 2
        + [pltpu.SemaphoreType.DMA((1,))],
        compiler_params=params(24),
        cost_estimate=pl.CostEstimate(
            flops=12 * height * cols * cols, bytes_accessed=16 * height * cols, transcendentals=0
        ),
    )(at, rows, table, side, base, lin_h, lin_l)
    return pieces, (spread_h, spread_l)


def finish_kernel(cuts, below, *refs):
    ins, (out, done, sems) = refs[:-3], refs[-3:]
    copies = []
    for c in range(done.shape[0]):
        for i, ref in enumerate(ins):
            rows = slice(cuts[i], cuts[i + 1])
            done[c, :, rows] = ref[:, c] / below[c, :, rows]
        copies.append(pltpu.make_async_copy(done.at[c], out.at[c], sems.at[c]))
        copies[-1].start()
    for copy in copies:
        copy.wait()


def finish(pieces, below, n, cuts):
    c, height, width = below.shape
    part = height // n
    sizes = [b - a for a, b in zip(cuts[:-1], cuts[1:])]
    shape = (c, n, part, width)
    return pl.pallas_call(
        functools.partial(finish_kernel, cuts),
        out_shape=pltpu.HBM(shape, F32),
        in_specs=[FULL] * (1 + len(pieces)),
        out_specs=pl.BlockSpec(memory_space=pltpu.HBM),
        scratch_shapes=[pltpu.VMEM(shape, F32), pltpu.SemaphoreType.DMA((c,))],
        compiler_params=params(12),
        cost_estimate=pl.CostEstimate(flops=c * height * width, bytes_accessed=12 * c * height * width, transcendentals=0),
    )(below.reshape(shape), *[p.reshape(n, c, rows, width) for p, rows in zip(pieces, sizes)]).reshape(below.shape)


def exchange(pieces, axes):
    return [lax.all_to_all(piece, axes, split_axis=0, concat_axis=0, tiled=True) for piece in pieces]


def per_device(amplitudes, interaction, sixj_values, sixj_index, ph_rows, denominators):
    c, height, width = amplitudes.shape
    n_chan, n_z = lax.axis_size("chan"), lax.axis_size("z")
    z, core = lax.axis_index("z"), lax.axis_index("core")
    at = jnp.reshape(z, (1,)).astype(jnp.int32)
    scale = 1.0 / (height * width * n_z * 2) ** 0.5

    def forward(core):
        def run(blocks, values, index):
            pieces, table, spread = deal(blocks, values, index, n_chan, FIRST[core])
            mixed = mix(spread, exchange(pieces, "chan"), (0, height // n_chan))
            return exchange(mixed, CHIPS)[0], table

        return run

    def backward(core):
        def run(at, rows, theirs, table, below, *sums):
            cycle, spread = other(at, rows, table, theirs, *sums, scale, THIRD[core])
            back = mix(spread, exchange(cycle, CHIPS), LAST[core])
            return finish(exchange(back, "chan"), below, n_chan, LAST[core])

        return run

    mine, table = lax.cond(core == 0, forward(0), forward(1), amplitudes, sixj_values, sixj_index)
    theirs = lax.ppermute(mine, "core", [(0, 1), (1, 0)])
    sums = own(at, ph_rows, mine, interaction, scale)
    return lax.cond(core == 0, backward(0), backward(1), at, ph_rows, theirs, table, denominators, *sums)


def solution(mesh):
    split = Mesh(mesh.devices.reshape(mesh.devices.shape[0], -1, 2), ("chan", "z", "core"))
    hole = ("z", "core")
    in_specs = (
        P("chan", None, hole),
        P("chan", None, None),
        P(),
        P(),
        P("chan"),
        P("chan", None, hole),
    )
    return jax.shard_map(
        per_device, mesh=split, in_specs=in_specs, out_specs=P("chan", None, hole), check_vma=False
    )
```

```python
import bisect
import functools
import jax
import jax.numpy as jnp
from jax import lax
from jax.experimental import pallas as pl
from jax.experimental.pallas import tpu as pltpu
from jax.sharding import Mesh, PartitionSpec as P

CHIPS = ("chan", "z")
FIRST = ((0, 64), (0, 16, 64))
THIRD = ((0, 64), (0, 8, 64))
LAST = ((0, 64), (0, 64))
MIB = 2**20
BF16, F32 = jnp.bfloat16, jnp.float32
ANY = pl.BlockSpec(memory_space=pl.ANY)
FULL = pl.BlockSpec(memory_space=pltpu.VMEM)
SCALAR = pl.BlockSpec(memory_space=pltpu.SMEM)
SUB = 8


def halves(x):
    high = x.astype(BF16)
    return high, (x - high.astype(F32)).astype(BF16)


def dot3(a, b, dims=((1,), (0,))):
    def one(x, y):
        return lax.dot_general(x, y, (dims, ((), ())), preferred_element_type=F32)

    return one(a[0], b[0]) + (one(a[0], b[1]) + one(a[1], b[0]))


def params(mib):
    return pltpu.CompilerParams(vmem_limit_bytes=mib * MIB)


def spread_table(table):
    n = table.shape[0]
    wide = n * SUB
    rows = (lax.broadcasted_iota(jnp.int32, (wide, n), 0) // SUB == lax.broadcasted_iota(jnp.int32, (wide, n), 1)).astype(BF16)
    columns = (lax.broadcasted_iota(jnp.int32, (n, wide), 1) // SUB == lax.broadcasted_iota(jnp.int32, (n, wide), 0)).astype(BF16)
    same = lax.broadcasted_iota(jnp.int32, (wide, wide), 0) % SUB == lax.broadcasted_iota(jnp.int32, (wide, wide), 1) % SUB
    spread = []
    for part in halves(table):
        tall = jnp.dot(rows, part, preferred_element_type=F32).astype(BF16)
        both = jnp.dot(tall, columns, preferred_element_type=F32)
        spread.append(jnp.where(same, both, 0.0).astype(BF16))
    return tuple(spread)


def deal_kernel(cuts, blocks, values, index, *refs):
    n_out = len(cuts) - 1
    outs, (table, spread_h, spread_l, slots, known, sems) = refs[:n_out], refs[n_out:]
    c = blocks.shape[0]
    copies = [
        pltpu.make_async_copy(blocks.at[i, :, pl.ds(cuts[k], cuts[k + 1] - cuts[k])], out.at[:, i], sems.at[k * c + i])
        for k, out in enumerate(outs)
        for i in range(c)
    ]
    small = [
        pltpu.make_async_copy(index, slots, sems.at[n_out * c]),
        pltpu.make_async_copy(values, known, sems.at[n_out * c + 1]),
    ]
    for copy in small + copies:
        copy.start()
    for copy in small:
        copy.wait()
    made = jnp.zeros(index.shape, F32)
    for slot in range(values.shape[0]):
        made = jnp.where(slots[...] == slot, known[slot], made)
    table[...] = made
    spread_h[...], spread_l[...] = spread_table(made)
    for copy in copies:
        copy.wait()


def deal(blocks, values, index, n, cuts):
    c, height, width = blocks.shape
    part = height // n
    sizes = [b - a for a, b in zip(cuts[:-1], cuts[1:])]
    wide = index.shape[0] * SUB
    sds = jax.ShapeDtypeStruct
    *pieces, table, spread_h, spread_l = pl.pallas_call(
        functools.partial(deal_kernel, cuts),
        out_shape=[sds((n, c, rows, width), F32) for rows in sizes]
        + [sds(index.shape, F32), sds((wide, wide), BF16), sds((wide, wide), BF16)],
        in_specs=[ANY] * 3,
        out_specs=[FULL] * (len(sizes) + 3),
        scratch_shapes=[
            pltpu.VMEM(index.shape, jnp.int32),
            pltpu.SMEM(values.shape, F32),
            pltpu.SemaphoreType.DMA((len(sizes) * c + 2,)),
        ],
        compiler_params=params(12),
        cost_estimate=pl.CostEstimate(flops=0, bytes_accessed=8 * c * height * width, transcendentals=0),
    )(blocks.reshape(c, n, part, width), values, index)
    return [piece.reshape(n * c, rows, width) for piece, rows in zip(pieces, sizes)], table, (spread_h, spread_l)


def mix_kernel(cuts, n_in, *refs):
    n_out = len(cuts) - 1
    given, pieces, outs = refs[:n_in], refs[n_in:-n_out], refs[-n_out:]
    n, _, width = outs[0].shape
    spread = spread_table(given[0][...].T) if n_in == 1 else tuple(ref[...] for ref in given)
    groups = [(ref, row) for ref in pieces for row in range(0, ref.shape[1], SUB)]
    for at in range(0, len(groups), 2):
        x = jnp.concatenate(
            [ref[:, row : row + SUB, :].reshape(n * SUB, width) for ref, row in groups[at : at + 2]], axis=1
        )
        y = dot3(spread, halves(x))
        for k in range(2):
            row = (at + k) * SUB
            i = bisect.bisect_right(cuts, row) - 1
            outs[i][:, row - cuts[i] : row - cuts[i] + SUB, :] = y[:, k * width : (k + 1) * width].reshape(n, SUB, width)


def mix(given, pieces, cuts):
    n, _, width = pieces[0].shape
    part = cuts[-1]
    return pl.pallas_call(
        functools.partial(mix_kernel, cuts, len(given)),
        out_shape=[jax.ShapeDtypeStruct((n, b - a, width), F32) for a, b in zip(cuts[:-1], cuts[1:])],
        in_specs=[FULL] * (len(given) + len(pieces)),
        out_specs=[FULL] * (len(cuts) - 1),
        compiler_params=params(16),
        cost_estimate=pl.CostEstimate(
            flops=6 * n * n * part * width * SUB, bytes_accessed=8 * n * part * width, transcendentals=0
        ),
    )(*given, *pieces)


def gather_side(ref, rows_of, scratch_high, scratch_low):
    n, part, width = ref.shape
    n_z = scratch_high.shape[1] // width
    for g in range(n // n_z):
        span = slice(g * part, (g + 1) * part)
        live = g * part + lax.broadcasted_iota(jnp.int32, (part, width), 0) < rows_of
        for k in range(n_z):
            high, low = halves(jnp.where(live, ref[g * n_z + k], 0.0))
            scratch_high[span, k * width : (k + 1) * width] = high
            scratch_low[span, k * width : (k + 1) * width] = low


def own_kernel(scale, block, at, rows, table, side, inter, acc, lin_h, lin_l, spread_h, spread_l, v, side_h, side_l, sem):
    height = v.shape[0]
    copies = [
        pltpu.make_async_copy(inter.at[at[0], pl.ds(r, block)], v.at[pl.ds(r, block)], sem.at[r // block])
        for r in range(0, height, block)
    ]
    for copy in copies:
        copy.start()
    gather_side(side, rows[at[0]], side_h, side_l)
    spread_h[...], spread_l[...] = spread_table(table[...].T)
    mine = (side_h[...], side_l[...])
    for r, copy in zip(range(0, height, block), copies):
        copy.wait()
        linear = dot3(halves(v[r : r + block]), mine)
        acc[r : r + block] = linear
        lin_h[r : r + block], lin_l[r : r + block] = halves(linear)
    inner = halves(dot3(mine, (lin_h[...], lin_l[...]), ((0,), (0,))) * scale)
    for r in range(0, height, block):
        acc[r : r + block] += dot3(tuple(s[r : r + block] for s in mine), inner)


def own(at, rows, table, side, inter, scale, block=256):
    n, part, width = side.shape
    height = inter.shape[1]
    cols = n * part * width // height
    wide = table.shape[0] * SUB
    sds = jax.ShapeDtypeStruct
    return pl.pallas_call(
        functools.partial(own_kernel, scale, block),
        out_shape=[sds((height, cols), F32), sds((height, cols), BF16), sds((height, cols), BF16)]
        + [sds((wide, wide), BF16)] * 2,
        in_specs=[SCALAR, SCALAR, FULL, FULL, ANY],
        out_specs=[FULL] * 5,
        scratch_shapes=[
            pltpu.VMEM((height, height), F32),
            pltpu.VMEM((height, cols), BF16),
            pltpu.VMEM((height, cols), BF16),
            pltpu.SemaphoreType.DMA((height // block,)),
        ],
        compiler_params=params(24),
        cost_estimate=pl.CostEstimate(
            flops=12 * height * height * cols, bytes_accessed=4 * height * (height + 3 * cols), transcendentals=0
        ),
    )(
        at,
        rows,
        table,
        pltpu.with_memory_space_constraint(side, pltpu.VMEM),
        pltpu.with_memory_space_constraint(inter, pltpu.HBM),
    )


def other_kernel(scale, cuts, at, rows, side, base, lin_h, lin_l, *refs):
    outs, (side_h, side_l) = refs[:-2], refs[-2:]
    n, part, width = side.shape
    n_z = side_h.shape[1] // width
    gather_side(side, rows[at[0]], side_h, side_l)
    theirs = (side_h[...], side_l[...])
    inner = halves(dot3(theirs, (lin_h[...], lin_l[...]), ((0,), (0,))) * scale)
    step = 4
    for g0 in range(0, n // n_z, step):
        span = slice(g0 * part, (g0 + step) * part)
        total = base[span] + dot3(tuple(s[span] for s in theirs), inner)
        live = g0 * part + lax.broadcasted_iota(jnp.int32, total.shape, 0) < rows[at[0]]
        total = jnp.where(live, total, 0.0)
        for g in range(step):
            for k in range(n_z):
                tile = total[g * part : (g + 1) * part, k * width : (k + 1) * width]
                for i, out in enumerate(outs):
                    out[(g0 + g) * n_z + k] = tile[cuts[i] : cuts[i + 1]]


def other(at, rows, side, base, lin_h, lin_l, scale, cuts):
    n, part, width = side.shape
    height, cols = base.shape
    return pl.pallas_call(
        functools.partial(other_kernel, scale, cuts),
        out_shape=[jax.ShapeDtypeStruct((n, b - a, width), F32) for a, b in zip(cuts[:-1], cuts[1:])],
        in_specs=[SCALAR, SCALAR] + [FULL] * 4,
        out_specs=[FULL] * (len(cuts) - 1),
        scratch_shapes=[pltpu.VMEM((height, cols), BF16)] * 2,
        compiler_params=params(24),
        cost_estimate=pl.CostEstimate(
            flops=12 * height * cols * cols, bytes_accessed=16 * height * cols, transcendentals=0
        ),
    )(at, rows, pltpu.with_memory_space_constraint(side, pltpu.VMEM), base, lin_h, lin_l)


def finish_kernel(cuts, below, *refs):
    ins, (out, done, sems) = refs[:-3], refs[-3:]
    copies = []
    for c in range(done.shape[0]):
        for i, ref in enumerate(ins):
            rows = slice(cuts[i], cuts[i + 1])
            done[c, :, rows] = ref[:, c] / below[c, :, rows]
        copies.append(pltpu.make_async_copy(done.at[c], out.at[c], sems.at[c]))
        copies[-1].start()
    for copy in copies:
        copy.wait()


def finish(pieces, below, n, cuts):
    c, height, width = below.shape
    part = height // n
    sizes = [b - a for a, b in zip(cuts[:-1], cuts[1:])]
    shape = (c, n, part, width)
    return pl.pallas_call(
        functools.partial(finish_kernel, cuts),
        out_shape=pltpu.HBM(shape, F32),
        in_specs=[FULL] * (1 + len(pieces)),
        out_specs=pl.BlockSpec(memory_space=pltpu.HBM),
        scratch_shapes=[pltpu.VMEM(shape, F32), pltpu.SemaphoreType.DMA((c,))],
        compiler_params=params(12),
        cost_estimate=pl.CostEstimate(flops=c * height * width, bytes_accessed=12 * c * height * width, transcendentals=0),
    )(below.reshape(shape), *[p.reshape(n, c, rows, width) for p, rows in zip(pieces, sizes)]).reshape(below.shape)


def exchange(pieces, axes):
    return [lax.all_to_all(piece, axes, split_axis=0, concat_axis=0, tiled=True) for piece in pieces]


def per_device(amplitudes, interaction, sixj_values, sixj_index, ph_rows, denominators):
    c, height, width = amplitudes.shape
    n_chan, n_z = lax.axis_size("chan"), lax.axis_size("z")
    z, core = lax.axis_index("z"), lax.axis_index("core")
    at = jnp.reshape(z, (1,)).astype(jnp.int32)
    scale = 1.0 / (height * width * n_z * 2) ** 0.5

    def forward(core):
        def run(blocks, values, index):
            pieces, table, spread = deal(blocks, values, index, n_chan, FIRST[core])
            mixed = mix(spread, exchange(pieces, "chan"), (0, height // n_chan))
            return exchange(mixed, CHIPS)[0], table

        return run

    def backward(core):
        def run(at, rows, theirs, spread, below, *sums):
            cycle = other(at, rows, theirs, *sums, scale, THIRD[core])
            back = mix(spread, exchange(cycle, CHIPS), LAST[core])
            return finish(exchange(back, "chan"), below, n_chan, LAST[core])

        return run

    mine, table = lax.cond(core == 0, forward(0), forward(1), amplitudes, sixj_values, sixj_index)
    theirs = lax.ppermute(mine, "core", [(0, 1), (1, 0)])
    *sums, spread_h, spread_l = own(at, ph_rows, table, mine, interaction, scale)
    spread = (spread_h, spread_l)
    return lax.cond(core == 0, backward(0), backward(1), at, ph_rows, theirs, spread, denominators, *sums)


def solution(mesh):
    split = Mesh(mesh.devices.reshape(mesh.devices.shape[0], -1, 2), ("chan", "z", "core"))
    hole = ("z", "core")
    in_specs = (
        P("chan", None, hole),
        P("chan", None, None),
        P(),
        P(),
        P("chan"),
        P("chan", None, hole),
    )
    return jax.shard_map(
        per_device, mesh=split, in_specs=in_specs, out_specs=P("chan", None, hole), check_vma=False
    )
```
